256 devices in a mesh: leaf: 64 (over x, z, core), vec: 4 (over y).
Axes of the slice: x: 4, y: 4, z: 8, core: 2. Of those that a mesh axis runs over, the one named last changes fastest.
Arguments:
- panels: float32 [32, 524288], P('vec', 'leaf'), may hold values from -6 to 6
- near_tiles: float32 [4096, 4, 128, 128], P('leaf', None, 'vec'), may hold values from -0.25 to 0.25
- near_cols: int32 [4096, 4], P('leaf'), may hold values from 0 to 4095, as said below
- leaf_order: int32 [4096, 128], P('leaf'), may hold values from 0 to 127, each once within a row
- leaf_basis: float32 [4096, 64, 128], P('leaf'), may hold values from -0.5 to 0.5
- local_mats: float32 [64, 63, 64, 128], P('leaf'), may hold values from -0.75 to 0.75
- local_flags: int32 [64, 63], P('leaf'), may hold values 0 or 1
- cross_coupling: float32 [62, 64, 64], replicated, may hold values from -0.75 to 0.75
- cross_transfer: float32 [60, 64, 64], replicated, may hold values from -0.75 to 0.75
- cross_flags: int32 [62], replicated, may hold values 0 or 1
Outputs:
- product: float32 [32, 524288], P('vec', 'leaf')
The draws below stay inside these ranges and needn't reach their ends.
Inputs may be any that keep to these rules, and one draw needn't show every extreme that they name: `near_cols`: every entry of row i names a leaf within 8 leaves of leaf i. `leaf_order`: each row is a permutation of 0 to 127.
All inputs are finite; a program needn't handle non-finite values. No bound on the sum of `local_flags` on one device may be relied on, other than what follows from the above.
Results may differ from the reference program's by a relative error of at most 0.00022.
Values sent between devices are 32-bit elements; how exact they have to be, the bound alone decides.
No kernel may reach another device: no remote copies, remote signals or barrier semaphores. Data moves between devices by JAX's collectives and lax.ppermute only.
A program may use at most 64 MiB of HBM per device.

```python
import math
import jax
import jax.numpy as jnp
from jax import lax

M = 128
K = 64
R = 32
NEAR = 4
W = 8
LEAF_DEV = 64
LEAVES = 4096
PANELS = 524288
LOCAL_DEPTH = 6
LEAF_DEPTH = 6
N_LEAF = 64


def draw_near_cols(key, part):
    row_ids = jnp.arange(LEAVES, dtype=jnp.int32)[:, None]
    offsets = jax.random.randint(key, (LEAVES, NEAR), -W, W + 1, dtype=jnp.int32)
    offsets = offsets.at[0, 0].set(W).at[LEAVES - 1, 0].set(-W)
    return jnp.clip(row_ids + offsets, 0, LEAVES - 1).astype(jnp.int32)


def touch_ends(values, key, smallest, largest):
    spot = [jax.random.randint(jax.random.fold_in(key, axis), (), 0, length) for axis, length in enumerate(values.shape)]
    widest = values.shape.index(max(values.shape))
    next_to = spot[:widest] + [(spot[widest] + 1) % values.shape[widest]] + spot[widest + 1:]
    return values.at[tuple(spot)].set(smallest).at[tuple(next_to)].set(largest)


def steps_of(stream_key, shape, shards, low, top_value):
    def one(axis_at, blocks):
        draws = jax.random.uniform(jax.random.fold_in(jax.random.fold_in(stream_key, 6), axis_at), (blocks,), jnp.float32, low / len(shards), top_value / len(shards))
        return jnp.repeat(jnp.exp(draws), shape[axis_at] // blocks).reshape((-1,) + (1,) * (len(shape) - axis_at - 1))

    factor_of = one(*shards[0])
    for cut in shards[1:]:
        factor_of = factor_of * one(*cut)
    return factor_of


def scatter_about(stream_key, extent, scale, limit, split=(), kind=jnp.bfloat16):
    values = jax.random.normal(stream_key, extent, jnp.float32) * scale
    if len(split) > 0:
        values = steps_of(stream_key, extent, split, -0.22, 0.18) * values
    return jnp.clip(values, min=-limit, max=limit).astype(kind)


def setup_inputs(seed: int = 0) -> dict:
    splits = jax.random.split(jax.random.key(seed), 11)
    panels = scatter_about(splits[0], (R, PANELS), 1.0, 6.0, ((0, 4), (1, 64)), jnp.float32)
    near_tiles = scatter_about(splits[1], (LEAVES, NEAR, M, M), (NEAR * M) ** -0.5, 0.25, ((0, 64), (2, 4)), jnp.float32)
    near_cols = draw_near_cols(jax.random.fold_in(splits[10], 71), 0)
    leaf_order = jax.vmap(lambda own: jax.random.permutation(own, M))(jax.random.split(splits[3], LEAVES)).reshape((LEAVES, M)).astype(jnp.int32)
    leaf_basis = scatter_about(splits[4], (LEAVES, K, M), M ** -0.5, 0.5, ((0, 64),), jnp.float32)
    local_mats = scatter_about(splits[5], (LEAVES // LEAF_DEV, LEAF_DEV - 1, K, 2 * K), K ** -0.5, 0.75, ((0, 64),), jnp.float32)
    local_flags = touch_ends((jax.random.randint(splits[6], (LEAVES // LEAF_DEV, LEAF_DEV - 1), 0, 4) < 3).astype(jnp.int32), jax.random.fold_in(splits[6], 1), 0, 1)
    cross_coupling = scatter_about(splits[7], (LEAVES // LEAF_DEV - 2, K, K), K ** -0.5, 0.75, (), jnp.float32)
    cross_transfer = scatter_about(splits[8], (LEAVES // LEAF_DEV - 4, K, K), K ** -0.5, 0.75, (), jnp.float32)
    cross_flags = touch_ends((jax.random.randint(splits[9], (LEAVES // LEAF_DEV - 2,), 0, 4) < 3).astype(jnp.int32), jax.random.fold_in(splits[9], 1), 0, 1)
    return dict(panels=panels, near_tiles=near_tiles, near_cols=near_cols, leaf_order=leaf_order, leaf_basis=leaf_basis, local_mats=local_mats, local_flags=local_flags, cross_coupling=cross_coupling, cross_transfer=cross_transfer, cross_flags=cross_flags)


precise = lax.Precision.HIGHEST
root_half = 1.0 / math.sqrt(2.0)

def swap_pairs(nodes):
    halves = nodes.reshape((nodes.shape[0] // 2, 2) + nodes.shape[1:])
    return halves[:, ::-1].reshape(nodes.shape)

def level_blocks(tree_level, local_mats, local_flags, cross_coupling, cross_transfer, cross_flags):
    if tree_level <= LOCAL_DEPTH:
        per_device = LEAF_DEV // 2 ** tree_level
        first_node = LEAF_DEV - LEAF_DEV // 2 ** (tree_level - 1)
        blocks = local_mats[:, first_node:first_node + per_device].reshape(N_LEAF * per_device, K, 2 * K)
        admits = local_flags[:, first_node:first_node + per_device].reshape(N_LEAF * per_device)
        return (blocks[:, :, :K], blocks[:, :, K:], admits)
    cross_level = tree_level - LOCAL_DEPTH
    node_count = N_LEAF // 2 ** cross_level
    first_node = N_LEAF - N_LEAF // 2 ** (cross_level - 1)
    couplings = cross_coupling[first_node:first_node + node_count]
    admits = cross_flags[first_node:first_node + node_count]
    if cross_level <= LEAF_DEPTH - 2:
        return (couplings, cross_transfer[first_node:first_node + node_count], admits)
    return (couplings, couplings, admits)

def reference(panels, near_tiles, near_cols, leaf_order, leaf_basis, local_mats, local_flags, cross_coupling, cross_transfer, cross_flags):
    rhs_count = panels.shape[0]
    order_full = jnp.broadcast_to(leaf_order[None], (rhs_count, LEAVES, M))
    ordered = jnp.take_along_axis(panels.reshape(rhs_count, LEAVES, M), order_full, axis=2)

    def near_block(block_pair):
        tile_block, columns = block_pair
        sources = ordered[:, columns]
        return jnp.einsum('lnqp,slnp->slq', tile_block, sources, precision=precise)
    blocks = lax.map(near_block, (near_tiles.reshape(N_LEAF, LEAF_DEV, NEAR, M, M), near_cols.reshape(N_LEAF, LEAF_DEV, NEAR)))
    near_field = jnp.transpose(blocks, (1, 0, 2, 3)).reshape(rhs_count, LEAVES, M)
    leaf_skel = jnp.einsum('lkp,slp->lsk', leaf_basis, ordered, precision=precise)
    skeleton = leaf_skel.reshape(LEAVES // 2, 2, rhs_count, K).sum(axis=1) * root_half
    top_level = LOCAL_DEPTH + LEAF_DEPTH - 1
    coupled = []
    transfers = []
    for tree_level in range(1, top_level + 1):
        couplings, transfer, admits = level_blocks(tree_level, local_mats, local_flags, cross_coupling, cross_transfer, cross_flags)
        term = jnp.einsum('jkm,jsm->jsk', couplings, swap_pairs(skeleton), precision=precise)
        coupled.append(admits.astype(jnp.float32)[:, None, None] * term)
        transfers.append(transfer)
        if tree_level < top_level:
            lifted = jnp.einsum('jsk,jkm->jsm', skeleton, transfer, precision=precise)
            skeleton = lifted.reshape(lifted.shape[0] // 2, 2, rhs_count, K).sum(axis=1) * root_half
    downward = coupled[top_level - 1]
    for tree_level in range(top_level - 1, 0, -1):
        spread = jnp.repeat(downward, 2, axis=0)
        downward = coupled[tree_level - 1] + jnp.einsum('jkm,jsm->jsk', transfers[tree_level - 1], spread, precision=precise)
    far_field = jnp.einsum('lkp,lsk->slp', leaf_basis, jnp.repeat(downward, 2, axis=0), precision=precise)
    combined = near_field + far_field
    inverse = jnp.argsort(leaf_order, axis=1).astype(jnp.int32)
    restored = jnp.take_along_axis(combined, jnp.broadcast_to(inverse[None], (rhs_count, LEAVES, M)), axis=2)
    return restored.reshape(rhs_count, PANELS)
```

```python
import math

import jax
import jax.numpy as jnp
from jax import lax
from jax.experimental import pallas as pl
from jax.experimental.pallas import tpu as pltpu
from jax.sharding import PartitionSpec as P

W = 8
ROOT_HALF = 1.0 / math.sqrt(2.0)
F32, BF16 = jnp.float32, jnp.bfloat16
NN = (((1,), (0,)), ((), ()))
NT = (((1,), (1,)), ((), ()))


def params():
    return pltpu.CompilerParams(vmem_limit_bytes=48 * 1024 * 1024)


def vmem():
    return pl.BlockSpec(memory_space=pltpu.VMEM)


def smem():
    return pl.BlockSpec(memory_space=pltpu.SMEM)


def halves(x):
    hi = x.astype(BF16).astype(F32)
    return hi, x - hi


def left_rows(x):
    hi, lo = halves(x)
    rows = jnp.concatenate([hi, lo], axis=0).astype(BF16)
    return jnp.concatenate([rows, rows], axis=1)


def mul_nn(x, w):
    m = x.shape[0]
    hi, lo = halves(w)
    both = jnp.concatenate([hi.astype(BF16), lo.astype(BF16)], axis=0)
    d = lax.dot_general(left_rows(x), both, NN, preferred_element_type=F32)
    return d[:m] + d[m:]


def mul_nt(x, w):
    m = x.shape[0]
    hi, lo = halves(w)
    both = jnp.concatenate([hi.astype(BF16), lo.astype(BF16)], axis=1)
    d = lax.dot_general(left_rows(x), both, NT, preferred_element_type=F32)
    return d[:m] + d[m:]


def lane_gather(x, index):
    return jnp.take_along_axis(x, index, axis=1, mode="promise_in_bounds")


def order_kernel(panels, order, ordered, head, tail):
    leaves = order.shape[0]
    for i in range(leaves):
        at = slice(128 * i, 128 * (i + 1))
        index = jnp.broadcast_to(order[i : i + 1, :], (panels.shape[0], 128))
        placed = lane_gather(panels[:, at], index)
        ordered[:, at] = placed
        if i < W:
            head[:, at] = placed
        if i >= leaves - W:
            j = i - (leaves - W)
            tail[:, 128 * j : 128 * (j + 1)] = placed


def inverse_kernel(order, inverse):
    leaves = order.shape[0]
    rows = lax.broadcasted_iota(jnp.int32, (128, 128), 0)
    places = lax.broadcasted_iota(jnp.int32, (16, 128), 1).astype(F32).astype(BF16)
    for i in range(leaves):
        hot = (jnp.broadcast_to(order[i : i + 1, :], (128, 128)) == rows).astype(F32).astype(BF16)
        inv = lax.dot_general(places, hot, NT, preferred_element_type=F32)
        inverse[i : i + 1, :] = inv[0:1].astype(jnp.int32)


def up_kernel(ordered, basis, mats, pairs, packets):
    leaves = basis.shape[0]
    rank = basis.shape[1]
    count = leaves // 2
    nodes = []
    for j in range(count):
        x = ordered[:, 256 * j : 256 * (j + 1)]
        w = jnp.concatenate([basis[2 * j], basis[2 * j + 1]], axis=1)
        nodes.append(mul_nt(x, w) * ROOT_HALF)
    first_pair, first_node = 0, 0
    while count > 1:
        lifted = []
        for j in range(count // 2):
            pair = jnp.concatenate([nodes[2 * j], nodes[2 * j + 1]], axis=1)
            pairs[first_pair + j] = pair
            at = first_node + 2 * j
            w = mats[at : at + 2].reshape(2 * rank, 2 * rank)
            lifted.append(mul_nn(pair, w)[:, rank:] * ROOT_HALF)
        nodes = lifted
        first_pair += count // 2
        first_node += count
        count //= 2
    skel = nodes[0]
    lift = mul_nn(skel, mats[first_node])[:, rank:]
    packet = jnp.concatenate([skel, lift], axis=1)
    packets[...] = jnp.broadcast_to(packet[None], packets.shape)


def near_kernel(cols, own, arr1, arr2, arr3, rim0, rim1, rim2, rim3, tiles, out0, out1, out2, out3, held):
    leaves = tiles.shape[0]
    slots = tiles.shape[1]
    base = lax.axis_index("leaf") * leaves - W
    mains = (own, arr1, arr2, arr3)
    rims = (rim0, rim1, rim2, rim3)
    outs = (out0, out1, out2, out3)

    def hold(place, refs, column):
        at = pl.ds(column, 128)
        x = jnp.concatenate([ref[:, at] for ref in refs], axis=0)
        hi, lo = halves(x)
        held[place] = jnp.concatenate([hi.astype(BF16), lo.astype(BF16)], axis=0)

    for i in range(W):
        hold(i, rims, 128 * i)
        hold(i + W + leaves, rims, 128 * (i + W))

    def hold_main(i, carry):
        hold(i + W, mains, pl.multiple_of(i * 128, 128))
        return carry

    lax.fori_loop(0, leaves, hold_main, 0, unroll=8)

    def group(g, carry):
        parts = []
        for k in range(4):
            i = 4 * g + k
            x = jnp.concatenate([held[cols[i, n] - base] for n in range(slots)], axis=1)
            t = jnp.concatenate([tiles[i, n] for n in range(slots)], axis=1)
            hi, lo = halves(t)
            w = jnp.concatenate([hi.astype(BF16), lo.astype(BF16)], axis=0)
            d = lax.dot_general(x, w, NT, preferred_element_type=F32)
            m, q = d.shape[0] // 2, d.shape[1] // 2
            parts.append(d[:m, :q] + (d[:m, q:] + d[m:, :q]))
        rows = jnp.concatenate(parts, axis=1)
        at = pl.ds(pl.multiple_of(g * 128, 128), 128)
        for k in range(4):
            outs[k][:, at] = rows[8 * k : 8 * (k + 1)]
        return carry

    lax.fori_loop(0, leaves // 4, group, 0, unroll=2)


def down_kernel(cross_flags, flags, packets, pairs, basis, mats, coupling, transfer, far, skels):
    leaves = basis.shape[0]
    rank = basis.shape[1]
    devices = packets.shape[0]
    me = lax.axis_index("leaf")
    count = devices // 2
    nodes = [
        (packets[2 * j][:, rank:] + packets[2 * j + 1][:, rank:]) * ROOT_HALF for j in range(count)
    ]
    first = 0
    while count > 1:
        for j in range(count):
            skels[first + j] = nodes[j]
        if count > 2:
            lifted = []
            for j in range(count // 2):
                pair = jnp.concatenate([nodes[2 * j], nodes[2 * j + 1]], axis=1)
                at = first + 2 * j
                w = transfer[at : at + 2].reshape(2 * rank, rank)
                lifted.append(mul_nn(pair, w) * ROOT_HALF)
            nodes = lifted
        first += count
        count //= 2
    depth = devices.bit_length() - 1
    z = None
    for c in range(depth - 1, 0, -1):
        start = devices - (devices >> (c - 1))
        node = start + (me >> c)
        sibling = start + ((me >> c) ^ 1)
        x = skels[sibling] * cross_flags[node].astype(F32)
        w = coupling[node]
        if z is None:
            z = mul_nt(x, w)
        else:
            z = mul_nt(x, w) + mul_nt(z, transfer[node])
    top = leaves - 2
    x = jnp.concatenate([packets[me ^ 1][:, :rank] * flags[0, top].astype(F32), z], axis=1)
    zs = [mul_nt(x, mats[top])]
    count = 2
    while count < leaves:
        first_node = leaves - 2 * count
        first_pair = (leaves - 2 * count) // 2
        lower = []
        for j in range(count // 2):
            pair = pairs[first_pair + j]
            z = zs[j]
            for side in (0, 1):
                node = first_node + 2 * j + side
                other = pair[:, rank:] if side == 0 else pair[:, :rank]
                x = jnp.concatenate([other * flags[0, node].astype(F32), z], axis=1)
                lower.append(mul_nt(x, mats[node]))
        zs = lower
        count *= 2
    for j in range(leaves // 2):
        w = jnp.concatenate([basis[2 * j], basis[2 * j + 1]], axis=1)
        both = mul_nn(zs[j], w)
        far[:, 256 * j : 256 * (j + 1)] = both


def final_kernel(inverse, far, near0, near1, near2, near3, out):
    leaves = inverse.shape[0]
    me = lax.axis_index("vec")
    nears = (near0, near1, near2, near3)
    for i in range(leaves):
        index = jnp.broadcast_to(inverse[i : i + 1, :], (out.shape[0], 128))
        owner = ((index >> 5) - me) & 3
        place = (index & 31) + 32 * (i % 4)
        at = slice(128 * (i // 4), 128 * (i // 4 + 1))
        near = lane_gather(near0[:, at], place)
        for k in (1, 2, 3):
            near = jnp.where(owner == k, lane_gather(nears[k][:, at], place), near)
        spot = slice(128 * i, 128 * (i + 1))
        out[:, spot] = near + lane_gather(far[:, spot], index)


def call(kernel, ins, out_shapes, scratch=(), scalars=0):
    return pl.pallas_call(
        kernel,
        out_shape=[jax.ShapeDtypeStruct(s, t) for s, t in out_shapes],
        in_specs=[smem()] * scalars + [vmem()] * (len(ins) - scalars),
        out_specs=[vmem()] * len(out_shapes),
        scratch_shapes=list(scratch),
        compiler_params=params(),
    )(*ins)


def local(
    panels,
    near_tiles,
    near_cols,
    leaf_order,
    leaf_basis,
    local_mats,
    local_flags,
    cross_coupling,
    cross_transfer,
    cross_flags,
):
    rhs = panels.shape[0]
    leaves, rank, size = leaf_basis.shape
    devices = lax.axis_size("leaf")
    parts = lax.axis_size("vec")
    mats = local_mats[0]
    rim = W * size

    def turned(x, k):
        return lax.ppermute(x, "vec", [(i, (i + k) % parts) for i in range(parts)])

    ordered, head, tail = call(
        order_kernel,
        (panels, leaf_order),
        [((rhs, leaves * size), F32), ((rhs, rim), F32), ((rhs, rim), F32)],
    )
    ends = devices - 1
    before = lax.ppermute(tail, "leaf", [(i, i + 1) for i in range(ends)])
    after = lax.ppermute(head, "leaf", [(i + 1, i) for i in range(ends)])
    others = [turned(ordered, k) for k in (1, 2, 3)]
    rims = jnp.concatenate([before, after], axis=1)
    other_rims = [turned(rims, k) for k in (1, 2, 3)]

    pairs, packets = call(
        up_kernel,
        (ordered, leaf_basis, mats),
        [((leaves // 2 - 1, rhs, 2 * rank), F32), ((devices, rhs, 2 * rank), F32)],
    )
    gathered = lax.all_to_all(packets, "leaf", 0, 0)
    (inverse,) = call(inverse_kernel, (leaf_order,), [((leaves, size), jnp.int32)])

    near = call(
        near_kernel,
        (near_cols, ordered, *others, rims, *other_rims, near_tiles),
        [((rhs, leaves * near_tiles.shape[2]), F32)] * 4,
        scratch=[pltpu.VMEM((leaves + 2 * W, 2 * parts * rhs, size), BF16)],
        scalars=1,
    )
    back = [near[0]] + [turned(near[k], -k) for k in (1, 2, 3)]

    (far,) = call(
        down_kernel,
        (cross_flags, local_flags, gathered, pairs, leaf_basis, mats, cross_coupling, cross_transfer),
        [((rhs, leaves * size), F32)],
        scratch=[pltpu.VMEM((devices - 2, rhs, rank), F32)],
        scalars=2,
    )
    (out,) = call(final_kernel, (inverse, far, *back), [((rhs, leaves * size), F32)])
    return out


def solution(mesh):
    return jax.shard_map(
        local,
        mesh=mesh,
        in_specs=(
            P("vec", "leaf"),
            P("leaf", None, "vec", None),
            P("leaf", None),
            P("leaf", None),
            P("leaf", None, None),
            P("leaf", None, None, None),
            P("leaf", None),
            P(),
            P(),
            P(),
        ),
        out_specs=P("vec", "leaf"),
        check_vma=False,
    )
```

```python
import math

import jax
import jax.numpy as jnp
from jax import lax
from jax.experimental import pallas as pl
from jax.experimental.pallas import tpu as pltpu
from jax.sharding import PartitionSpec as P

W = 8
NEAR_US = 5
EARLY = 1
MIB = 52
MIB0 = 52
ROOT_HALF = 1.0 / math.sqrt(2.0)
F32, BF16 = jnp.float32, jnp.bfloat16
NN = (((1,), (0,)), ((), ()))
NT = (((1,), (1,)), ((), ()))


def params(mib):
    return pltpu.CompilerParams(vmem_limit_bytes=int(mib * 1024 * 1024))


def vmem():
    return pl.BlockSpec(memory_space=pltpu.VMEM)


def smem():
    return pl.BlockSpec(memory_space=pltpu.SMEM)


def hbm():
    return pl.BlockSpec(memory_space=pltpu.HBM)


def halves(x):
    hi = x.astype(BF16).astype(F32)
    return hi, x - hi


def left_rows(x):
    hi, lo = halves(x)
    rows = jnp.concatenate([hi, lo], axis=0).astype(BF16)
    return jnp.concatenate([rows, rows], axis=1)


def mul_nn(x, w):
    m = x.shape[0]
    hi, lo = halves(w)
    both = jnp.concatenate([hi.astype(BF16), lo.astype(BF16)], axis=0)
    d = lax.dot_general(left_rows(x), both, NN, preferred_element_type=F32)
    return d[:m] + d[m:]


def mul_nt(x, w):
    m = x.shape[0]
    hi, lo = halves(w)
    both = jnp.concatenate([hi.astype(BF16), lo.astype(BF16)], axis=1)
    d = lax.dot_general(left_rows(x), both, NT, preferred_element_type=F32)
    return d[:m] + d[m:]


def lane_gather(x, index):
    return jnp.take_along_axis(x, index, axis=1, mode="promise_in_bounds")


def order_kernel(panels_hbm, order_hbm, middle, head, tail, panels, order, sems):
    copies = [
        pltpu.make_async_copy(order_hbm, order, sems.at[0]),
        pltpu.make_async_copy(panels_hbm, panels, sems.at[1]),
    ]
    for copy in copies:
        copy.start()
    for copy in copies:
        copy.wait()
    leaves = order.shape[0]
    for i in range(leaves):
        index = jnp.broadcast_to(order[i : i + 1, :], (panels.shape[0], 128))
        placed = lane_gather(panels[:, 128 * i : 128 * (i + 1)], index)
        middle[:, 128 * (i + W) : 128 * (i + W + 1)] = placed
        if i < W:
            head[:, 128 * i : 128 * (i + 1)] = placed
        if i >= leaves - W:
            j = i - (leaves - W)
            tail[:, 128 * j : 128 * (j + 1)] = placed


def rim_kernel(middle, before, after, extended):
    del middle
    width = before.shape[1]
    extended[:, :width] = before[...]
    extended[:, extended.shape[1] - width :] = after[...]


def inverse_kernel(order, inverse):
    leaves = order.shape[0]
    rows = lax.broadcasted_iota(jnp.int32, (128, 128), 0)
    places = lax.broadcasted_iota(jnp.int32, (16, 128), 1).astype(F32).astype(BF16)
    for i in range(leaves):
        hot = (jnp.broadcast_to(order[i : i + 1, :], (128, 128)) == rows).astype(F32).astype(BF16)
        inv = lax.dot_general(places, hot, NT, preferred_element_type=F32)
        inverse[i : i + 1, :] = inv[0:1].astype(jnp.int32)


def up_kernel(middle, basis_hbm, mats_hbm, pairs, packets, basis, mats, basis_sems, mats_sems):
    leaves = basis.shape[0]
    rank = basis.shape[1]
    count = leaves // 2
    nodes = []
    chunks = basis_sems.shape[0]
    basis_copies = chunked(basis_hbm, basis, basis_sems, chunks)
    mats_copies = chunked(mats_hbm, mats, mats_sems, 2)
    for j in range(count):
        if j % (count // chunks) == 0:
            basis_copies[j // (count // chunks)].wait()
        x = middle[:, 128 * (2 * j + W) : 128 * (2 * j + 2 + W)]
        w = jnp.concatenate([basis[2 * j], basis[2 * j + 1]], axis=1)
        nodes.append(mul_nt(x, w) * ROOT_HALF)
    first_pair, first_node = 0, 0
    mats_copies[0].wait()
    while count > 1:
        if first_node == leaves // 2:
            mats_copies[1].wait()
        lifted = []
        for j in range(count // 2):
            pair = jnp.concatenate([nodes[2 * j], nodes[2 * j + 1]], axis=1)
            pairs[first_pair + j] = pair
            at = first_node + 2 * j
            w = mats[at : at + 2].reshape(2 * rank, 2 * rank)
            lifted.append(mul_nn(pair, w)[:, rank:] * ROOT_HALF)
        nodes = lifted
        first_pair += count // 2
        first_node += count
        count //= 2
    skel = nodes[0]
    lift = mul_nn(skel, mats[first_node])[:, rank:]
    packet = jnp.concatenate([skel, lift], axis=1)
    packets[...] = jnp.broadcast_to(packet[None], packets.shape)


def near_kernel(cols, own, arr1, arr2, arr3, tiles_hbm, out0, out1, out2, out3, held, tiles, sems):
    copies = chunked(tiles_hbm, tiles, sems, 4)
    leaves = tiles.shape[0]
    slots = tiles.shape[1]
    base = lax.axis_index("leaf") * leaves - W
    outs = (out0, out1, out2, out3)

    def hold(i, carry):
        at = pl.ds(pl.multiple_of(i * 128, 128), 128)
        x = jnp.concatenate([ref[:, at] for ref in (own, arr1, arr2, arr3)], axis=0)
        hi, lo = halves(x)
        held[i] = jnp.concatenate([hi.astype(BF16), lo.astype(BF16)], axis=0)
        return carry

    lax.fori_loop(0, leaves + 2 * W, hold, 0, unroll=8)

    def group(g, carry):
        parts = []
        for k in range(4):
            i = 4 * g + k
            x = jnp.concatenate([held[cols[n, i] - base] for n in range(slots)], axis=1)
            t = jnp.concatenate([tiles[i, n] for n in range(slots)], axis=1)
            hi, lo = halves(t)
            w = jnp.concatenate([hi.astype(BF16), lo.astype(BF16)], axis=0)
            d = lax.dot_general(x, w, NT, preferred_element_type=F32)
            m, q = d.shape[0] // 2, d.shape[1] // 2
            parts.append(d[:m, :q] + (d[:m, q:] + d[m:, :q]))
        rows = jnp.concatenate(parts, axis=1)
        at = pl.ds(pl.multiple_of(g * 128, 128), 128)
        for k in range(4):
            outs[k][:, at] = rows[8 * k : 8 * (k + 1)]
        return carry

    quarter = leaves // 16
    for c in range(4):
        copies[c].wait()
        lax.fori_loop(c * quarter, (c + 1) * quarter, group, 0, unroll=2)


def down_kernel(
    cross_flags, flags, packets, pairs, basis_hbm, mats_hbm, coupling_hbm, transfer_hbm,
    far, skels, basis, mats, coupling, transfer, sems,
):
    leaves = basis.shape[0]
    rank = basis.shape[1]
    devices = packets.shape[0]
    depth = devices.bit_length() - 1
    me = lax.axis_index("leaf")
    transfer_copy = pltpu.make_async_copy(transfer_hbm, transfer, sems.at[0])
    transfer_copy.start()
    coupling_copies = []
    for c in range(1, depth):
        node = devices - (devices >> (c - 1)) + (me >> c)
        coupling_copies.append(
            pltpu.make_async_copy(coupling_hbm.at[node], coupling.at[c - 1], sems.at[2 + c])
        )
        coupling_copies[-1].start()
    mats_copy = pltpu.make_async_copy(mats_hbm, mats, sems.at[1])
    mats_copy.start()
    basis_copy = pltpu.make_async_copy(basis_hbm, basis, sems.at[2])
    basis_copy.start()
    count = devices // 2
    nodes = [
        (packets[2 * j][:, rank:] + packets[2 * j + 1][:, rank:]) * ROOT_HALF for j in range(count)
    ]
    first = 0
    transfer_copy.wait()
    while count > 1:
        for j in range(count):
            skels[first + j] = nodes[j]
        if count > 2:
            lifted = []
            for j in range(count // 2):
                pair = jnp.concatenate([nodes[2 * j], nodes[2 * j + 1]], axis=1)
                at = first + 2 * j
                w = transfer[at : at + 2].reshape(2 * rank, rank)
                lifted.append(mul_nn(pair, w) * ROOT_HALF)
            nodes = lifted
        first += count
        count //= 2
    for copy in coupling_copies:
        copy.wait()
    z = None
    for c in range(depth - 1, 0, -1):
        start = devices - (devices >> (c - 1))
        node = start + (me >> c)
        sibling = start + ((me >> c) ^ 1)
        x = skels[sibling] * cross_flags[node].astype(F32)
        w = coupling[c - 1]
        if z is None:
            z = mul_nt(x, w)
        else:
            z = mul_nt(x, w) + mul_nt(z, transfer[node])
    top = leaves - 2
    x = jnp.concatenate([packets[me ^ 1][:, :rank] * flags[0, top].astype(F32), z], axis=1)
    mats_copy.wait()
    zs = [mul_nt(x, mats[top])]
    count = 2
    while count < leaves:
        first_node = leaves - 2 * count
        first_pair = (leaves - 2 * count) // 2
        lower = []
        for j in range(count // 2):
            pair = pairs[first_pair + j]
            z = zs[j]
            for side in (0, 1):
                node = first_node + 2 * j + side
                other = pair[:, rank:] if side == 0 else pair[:, :rank]
                x = jnp.concatenate([other * flags[0, node].astype(F32), z], axis=1)
                lower.append(mul_nt(x, mats[node]))
        zs = lower
        count *= 2
    basis_copy.wait()
    for j in range(leaves // 2):
        w = jnp.concatenate([basis[2 * j], basis[2 * j + 1]], axis=1)
        both = mul_nn(zs[j], w)
        far[:, 256 * j : 256 * (j + 1)] = both


def final_kernel(inverse, far, near0, near1, near2, near3, out):
    leaves = inverse.shape[0]
    me = lax.axis_index("vec")
    nears = (near0, near1, near2, near3)
    for i in range(leaves):
        index = jnp.broadcast_to(inverse[i : i + 1, :], (out.shape[0], 128))
        owner = ((index >> 5) - me) & 3
        place = (index & 31) + 32 * (i % 4)
        at = slice(128 * (i // 4), 128 * (i // 4 + 1))
        near = lane_gather(near0[:, at], place)
        for k in (1, 2, 3):
            near = jnp.where(owner == k, lane_gather(nears[k][:, at], place), near)
        spot = slice(128 * i, 128 * (i + 1))
        out[:, spot] = near + lane_gather(far[:, spot], index)


def call(kernel, spaces, ins, out_shapes, scratch=(), mib=0, us=0, alias={}):
    place = {"s": smem, "v": vmem, "h": hbm}
    return pl.pallas_call(
        kernel,
        out_shape=[jax.ShapeDtypeStruct(s, t) for s, t in out_shapes],
        in_specs=[place[k]() for k in spaces],
        out_specs=[vmem()] * len(out_shapes),
        scratch_shapes=list(scratch),
        input_output_aliases=alias,
        compiler_params=params(mib or MIB),
        cost_estimate=pl.CostEstimate(flops=int(us * 1.15e9), bytes_accessed=0, transcendentals=0) if us else None,
    )(*ins)


def chunked(source, target, sems, chunks):
    step = -(-source.shape[0] // chunks)
    copies = []
    for c in range(chunks):
        at = pl.ds(c * step, min(step, source.shape[0] - c * step))
        copies.append(pltpu.make_async_copy(source.at[at], target.at[at], sems.at[c]))
        copies[-1].start()
    return copies


def local(
    panels,
    near_tiles,
    near_cols,
    leaf_order,
    leaf_basis,
    local_mats,
    local_flags,
    cross_coupling,
    cross_transfer,
    cross_flags,
):
    rhs = panels.shape[0]
    leaves, rank, size = leaf_basis.shape
    devices = lax.axis_size("leaf")
    parts = lax.axis_size("vec")
    mats = local_mats[0]
    rim = W * size

    def turned(x, k):
        return lax.ppermute(x, "vec", [(i, (i + k) % parts) for i in range(parts)])

    dma = pltpu.SemaphoreType.DMA

    def up(source):
        return call(
            up_kernel,
            "vhh",
            (source, leaf_basis, mats),
            [((leaves // 2 - 1, rhs, 2 * rank), F32), ((devices, rhs, 2 * rank), F32)],
            [basis_shape, mats_shape, dma((8,)), dma((2,))],
        )

    basis_shape = pltpu.VMEM(leaf_basis.shape, F32)
    mats_shape = pltpu.VMEM(mats.shape, F32)
    length = (leaves + 2 * W) * size
    middle, head, tail = call(
        order_kernel,
        "hh",
        (panels, leaf_order),
        [((rhs, length), F32), ((rhs, rim), F32), ((rhs, rim), F32)],
        [pltpu.VMEM(panels.shape, F32), pltpu.VMEM(leaf_order.shape, jnp.int32), dma((2,))],
        MIB0,
    )
    ends = devices - 1
    before = lax.ppermute(tail, "leaf", [(i, i + 1) for i in range(ends)])
    after = lax.ppermute(head, "leaf", [(i + 1, i) for i in range(ends)])
    (inverse,) = call(inverse_kernel, "v", (leaf_order,), [((leaves, size), jnp.int32)])
    if EARLY:
        pairs, packets = up(middle)
        middle, before, after, packets = lax.optimization_barrier((middle, before, after, packets))
    if EARLY == 2:
        middle, before, after, inverse = lax.optimization_barrier((middle, before, after, inverse))
    (own,) = call(rim_kernel, "vvv", (middle, before, after), [((rhs, length), F32)], alias={0: 0})
    others = [turned(own, k) for k in (1, 2, 3)]
    if not EARLY:
        pairs, packets = up(own)
    gathered = lax.all_to_all(packets, "leaf", 0, 0)
    near = call(
        near_kernel,
        "svvvvh",
        (near_cols.T, own, *others, near_tiles),
        [((rhs, leaves * near_tiles.shape[2]), F32)] * 4,
        [
            pltpu.VMEM((leaves + 2 * W, 2 * parts * rhs, size), BF16),
            pltpu.VMEM(near_tiles.shape, F32),
            dma((4,)),
        ],
        0,
        NEAR_US,
    )
    back = [near[0]] + [turned(near[k], -k) for k in (1, 2, 3)]

    (far,) = call(
        down_kernel,
        "ssvvhhhh",
        (cross_flags, local_flags, gathered, pairs, leaf_basis, mats, cross_coupling, cross_transfer),
        [((rhs, leaves * size), F32)],
        [
            pltpu.VMEM((devices - 2, rhs, rank), F32),
            basis_shape,
            mats_shape,
            pltpu.VMEM((devices.bit_length() - 2, rank, rank), F32),
            pltpu.VMEM(cross_transfer.shape, F32),
            dma((devices.bit_length() + 2,)),
        ],
    )
    (out,) = call(final_kernel, "vvvvvv", (inverse, far, *back), [((rhs, leaves * size), F32)])
    return out


def solution(mesh):
    return jax.shard_map(
        local,
        mesh=mesh,
        in_specs=(
            P("vec", "leaf"),
            P("leaf", None, "vec", None),
            P("leaf", None),
            P("leaf", None),
            P("leaf", None, None),
            P("leaf", None, None, None),
            P("leaf", None),
            P(),
            P(),
            P(),
        ),
        out_specs=P("vec", "leaf"),
        check_vma=False,
    )
```

```python
import math

import jax
import jax.numpy as jnp
from jax import lax
from jax.experimental import pallas as pl
from jax.experimental.pallas import tpu as pltpu
from jax.sharding import PartitionSpec as P

W = 8
NEAR_US = 5
EARLY = 0
CHUNKS = 2
MCHUNKS = 1
UNROLL = 4
MIB = 52
MIB0 = 52
ROOT_HALF = 1.0 / math.sqrt(2.0)
F32, BF16 = jnp.float32, jnp.bfloat16
NN = (((1,), (0,)), ((), ()))
NT = (((1,), (1,)), ((), ()))


def params(mib):
    return pltpu.CompilerParams(vmem_limit_bytes=int(mib * 1024 * 1024))


def vmem():
    return pl.BlockSpec(memory_space=pltpu.VMEM)


def smem():
    return pl.BlockSpec(memory_space=pltpu.SMEM)


def hbm():
    return pl.BlockSpec(memory_space=pltpu.HBM)


def halves(x):
    hi = x.astype(BF16).astype(F32)
    return hi, x - hi


def left_rows(x):
    hi, lo = halves(x)
    rows = jnp.concatenate([hi, lo], axis=0).astype(BF16)
    return jnp.concatenate([rows, rows], axis=1)


def mul_nn(x, w):
    m = x.shape[0]
    hi, lo = halves(w)
    both = jnp.concatenate([hi.astype(BF16), lo.astype(BF16)], axis=0)
    d = lax.dot_general(left_rows(x), both, NN, preferred_element_type=F32)
    return d[:m] + d[m:]


def mul_nt(x, w):
    m = x.shape[0]
    hi, lo = halves(w)
    both = jnp.concatenate([hi.astype(BF16), lo.astype(BF16)], axis=1)
    d = lax.dot_general(left_rows(x), both, NT, preferred_element_type=F32)
    return d[:m] + d[m:]


def lane_gather(x, index):
    return jnp.take_along_axis(x, index, axis=1, mode="promise_in_bounds")


def order_kernel(panels_hbm, order_hbm, middle, near_rim, far_rim, panels, order, sems):
    copies = [
        pltpu.make_async_copy(order_hbm, order, sems.at[0]),
        pltpu.make_async_copy(panels_hbm, panels, sems.at[1]),
    ]
    even = (lax.axis_index("leaf") & 1) == 0
    for copy in copies:
        copy.start()
    for copy in copies:
        copy.wait()
    leaves = order.shape[0]
    first, last = [], []
    for i in range(leaves):
        at = slice(128 * i, 128 * (i + 1))
        index = jnp.broadcast_to(order[i : i + 1, :], (panels.shape[0], 128))
        placed = lane_gather(panels[:, at], index)
        middle[:, 128 * (i + W) : 128 * (i + W + 1)] = placed
        if i < W:
            first.append(placed)
        if i >= leaves - W:
            last.append(placed)
    for i in range(W):
        at = slice(128 * i, 128 * (i + 1))
        near_rim[:, at] = jnp.where(even, last[i], first[i])
        far_rim[:, at] = jnp.where(even, first[i], last[i])


def invert(order, inverse):
    leaves = order.shape[0]
    rows = lax.broadcasted_iota(jnp.int32, (128, 128), 0)
    places = lax.broadcasted_iota(jnp.int32, (16, 128), 1).astype(F32).astype(BF16)
    for i in range(leaves):
        hot = (jnp.broadcast_to(order[i : i + 1, :], (128, 128)) == rows).astype(F32).astype(BF16)
        inv = lax.dot_general(places, hot, NT, preferred_element_type=F32)
        inverse[i : i + 1, :] = inv[0:1].astype(jnp.int32)


def up_kernel(
    middle, near_rim, order, basis_hbm, mats_hbm, pairs, packet, inverse, basis, mats, basis_sems, mats_sems
):
    leaves = basis.shape[0]
    rank = basis.shape[1]
    count = leaves // 2
    nodes = []
    chunks = basis_sems.shape[0]
    basis_copies = chunked(basis_hbm, basis, basis_sems, chunks)
    mats_copies = chunked(mats_hbm, mats, mats_sems, mats_sems.shape[0])
    invert(order, inverse)
    for j in range(count):
        if j % (count // chunks) == 0:
            basis_copies[j // (count // chunks)].wait()
        x = middle[:, 128 * (2 * j + W) : 128 * (2 * j + 2 + W)]
        w = jnp.concatenate([basis[2 * j], basis[2 * j + 1]], axis=1)
        nodes.append(mul_nt(x, w) * ROOT_HALF)
    first_pair, first_node = 0, 0
    mats_copies[0].wait()
    while count > 1:
        if first_node == leaves // 2 and len(mats_copies) == 2:
            mats_copies[1].wait()
        lifted = []
        for j in range(count // 2):
            pair = jnp.concatenate([nodes[2 * j], nodes[2 * j + 1]], axis=1)
            pairs[first_pair + j] = pair
            at = first_node + 2 * j
            w = mats[at : at + 2].reshape(2 * rank, 2 * rank)
            lifted.append(mul_nn(pair, w)[:, rank:] * ROOT_HALF)
        nodes = lifted
        first_pair += count // 2
        first_node += count
        count //= 2
    skel = nodes[0]
    lift = mul_nn(skel, mats[first_node])[:, rank:]
    packet[:, : near_rim.shape[1]] = near_rim[...]
    packet[:, near_rim.shape[1] :] = jnp.concatenate([skel, lift], axis=1)


def join_kernel(middle, packet, other, far_rim, extended, packets):
    del middle
    even = (lax.axis_index("leaf") & 1) == 0
    width = far_rim.shape[1]
    near_rim = other[:, :width]
    extended[:, :width] = jnp.where(even, far_rim[...], near_rim)
    extended[:, extended.shape[1] - width :] = jnp.where(even, near_rim, far_rim[...])
    half = packets.shape[1]
    rank = packets.shape[2] // 2
    lift = width + rank
    node = (packet[:, lift:] + other[:, lift:]) * ROOT_HALF
    rows = jnp.concatenate([node[:half], node[half:]], axis=1)
    packets[...] = jnp.broadcast_to(rows[None], packets.shape)


def near_kernel(cols, own, arr1, arr2, arr3, tiles_hbm, out0, out1, out2, out3, held, tiles, sems):
    copies = chunked(tiles_hbm, tiles, sems, 4)
    leaves = tiles.shape[0]
    slots = tiles.shape[1]
    base = lax.axis_index("leaf") * leaves - W
    outs = (out0, out1, out2, out3)

    def hold(i, carry):
        at = pl.ds(pl.multiple_of(i * 128, 128), 128)
        x = jnp.concatenate([ref[:, at] for ref in (own, arr1, arr2, arr3)], axis=0)
        hi, lo = halves(x)
        held[i] = jnp.concatenate([hi.astype(BF16), lo.astype(BF16)], axis=0)
        return carry

    lax.fori_loop(0, leaves + 2 * W, hold, 0, unroll=8)

    def group(g, carry):
        parts = []
        for k in range(4):
            i = 4 * g + k
            x = jnp.concatenate([held[cols[n, i] - base] for n in range(slots)], axis=1)
            t = jnp.concatenate([tiles[i, n] for n in range(slots)], axis=1)
            hi, lo = halves(t)
            w = jnp.concatenate([hi.astype(BF16), lo.astype(BF16)], axis=0)
            d = lax.dot_general(x, w, NT, preferred_element_type=F32)
            m, q = d.shape[0] // 2, d.shape[1] // 2
            parts.append(d[:m, :q] + (d[:m, q:] + d[m:, :q]))
        rows = jnp.concatenate(parts, axis=1)
        at = pl.ds(pl.multiple_of(g * 128, 128), 128)
        for k in range(4):
            outs[k][:, at] = rows[8 * k : 8 * (k + 1)]
        return carry

    quarter = leaves // 16
    for c in range(4):
        copies[c].wait()
        lax.fori_loop(c * quarter, (c + 1) * quarter, group, 0, unroll=UNROLL)


def down_kernel(
    cross_flags, flags, packets, other, pairs, basis_hbm, mats_hbm, coupling_hbm, transfer_hbm,
    far, skels, basis, mats, coupling, transfer, sems,
):
    leaves = basis.shape[0]
    rank = basis.shape[1]
    devices = 2 * packets.shape[0]
    depth = devices.bit_length() - 1
    me = lax.axis_index("leaf")
    skel = other.shape[1] - 2 * rank
    transfer_copy = pltpu.make_async_copy(transfer_hbm, transfer, sems.at[0])
    transfer_copy.start()
    coupling_copies = []
    for c in range(1, depth):
        node = devices - (devices >> (c - 1)) + (me >> c)
        coupling_copies.append(
            pltpu.make_async_copy(coupling_hbm.at[node], coupling.at[c - 1], sems.at[2 + c])
        )
        coupling_copies[-1].start()
    mats_copy = pltpu.make_async_copy(mats_hbm, mats, sems.at[1])
    mats_copy.start()
    basis_copy = pltpu.make_async_copy(basis_hbm, basis, sems.at[2])
    basis_copy.start()
    count = devices // 2
    nodes = [
        jnp.concatenate([packets[j][:, :rank], packets[j][:, rank:]], axis=0) for j in range(count)
    ]
    first = 0
    transfer_copy.wait()
    while count > 1:
        for j in range(count):
            skels[first + j] = nodes[j]
        if count > 2:
            lifted = []
            for j in range(count // 2):
                pair = jnp.concatenate([nodes[2 * j], nodes[2 * j + 1]], axis=1)
                at = first + 2 * j
                w = transfer[at : at + 2].reshape(2 * rank, rank)
                lifted.append(mul_nn(pair, w) * ROOT_HALF)
            nodes = lifted
        first += count
        count //= 2
    for copy in coupling_copies:
        copy.wait()
    z = None
    for c in range(depth - 1, 0, -1):
        start = devices - (devices >> (c - 1))
        node = start + (me >> c)
        sibling = start + ((me >> c) ^ 1)
        x = skels[sibling] * cross_flags[node].astype(F32)
        w = coupling[c - 1]
        if z is None:
            z = mul_nt(x, w)
        else:
            z = mul_nt(x, w) + mul_nt(z, transfer[node])
    top = leaves - 2
    x = jnp.concatenate([other[:, skel : skel + rank] * flags[0, top].astype(F32), z], axis=1)
    mats_copy.wait()
    zs = [mul_nt(x, mats[top])]
    count = 2
    while count < leaves:
        first_node = leaves - 2 * count
        first_pair = (leaves - 2 * count) // 2
        lower = []
        for j in range(count // 2):
            pair = pairs[first_pair + j]
            z = zs[j]
            for side in (0, 1):
                node = first_node + 2 * j + side
                other = pair[:, rank:] if side == 0 else pair[:, :rank]
                x = jnp.concatenate([other * flags[0, node].astype(F32), z], axis=1)
                lower.append(mul_nt(x, mats[node]))
        zs = lower
        count *= 2
    basis_copy.wait()
    for j in range(leaves // 2):
        w = jnp.concatenate([basis[2 * j], basis[2 * j + 1]], axis=1)
        both = mul_nn(zs[j], w)
        far[:, 256 * j : 256 * (j + 1)] = both


def final_kernel(inverse, far, near0, near1, near2, near3, out_hbm, out, sems):
    leaves = inverse.shape[0]
    me = lax.axis_index("vec")
    nears = (near0, near1, near2, near3)
    copies = []
    chunk = leaves // sems.shape[0]
    for i in range(leaves):
        index = jnp.broadcast_to(inverse[i : i + 1, :], (out.shape[0], 128))
        owner = ((index >> 5) - me) & 3
        place = (index & 31) + 32 * (i % 4)
        at = slice(128 * (i // 4), 128 * (i // 4 + 1))
        near = lane_gather(near0[:, at], place)
        for k in (1, 2, 3):
            near = jnp.where(owner == k, lane_gather(nears[k][:, at], place), near)
        spot = slice(128 * i, 128 * (i + 1))
        out[:, spot] = near + lane_gather(far[:, spot], index)
        if (i + 1) % chunk == 0:
            c = i // chunk
            at = pl.ds(128 * chunk * c, 128 * chunk)
            copies.append(pltpu.make_async_copy(out.at[:, at], out_hbm.at[:, at], sems.at[c]))
            copies[-1].start()
    for copy in copies:
        copy.wait()


def call(kernel, spaces, ins, out_shapes, scratch=(), mib=0, us=0, out_space=vmem, alias={}):
    place = {"s": smem, "v": vmem, "h": hbm}
    return pl.pallas_call(
        kernel,
        out_shape=[jax.ShapeDtypeStruct(s, t) for s, t in out_shapes],
        in_specs=[place[k]() for k in spaces],
        out_specs=[out_space()] * len(out_shapes),
        scratch_shapes=list(scratch),
        input_output_aliases=alias,
        compiler_params=params(mib or MIB),
        cost_estimate=pl.CostEstimate(flops=int(us * 1.15e9), bytes_accessed=0, transcendentals=0) if us else None,
    )(*ins)


def chunked(source, target, sems, chunks):
    step = -(-source.shape[0] // chunks)
    copies = []
    for c in range(chunks):
        at = pl.ds(c * step, min(step, source.shape[0] - c * step))
        copies.append(pltpu.make_async_copy(source.at[at], target.at[at], sems.at[c]))
        copies[-1].start()
    return copies


def local(
    panels,
    near_tiles,
    near_cols,
    leaf_order,
    leaf_basis,
    local_mats,
    local_flags,
    cross_coupling,
    cross_transfer,
    cross_flags,
):
    rhs = panels.shape[0]
    leaves, rank, size = leaf_basis.shape
    devices = lax.axis_size("leaf")
    parts = lax.axis_size("vec")
    mats = local_mats[0]
    rim = W * size

    def turned(x, k):
        return lax.ppermute(x, "vec", [(i, (i + k) % parts) for i in range(parts)])

    dma = pltpu.SemaphoreType.DMA

    basis_shape = pltpu.VMEM(leaf_basis.shape, F32)
    mats_shape = pltpu.VMEM(mats.shape, F32)
    length = (leaves + 2 * W) * size
    middle, near_rim, far_rim = call(
        order_kernel,
        "hh",
        (panels, leaf_order),
        [((rhs, length), F32), ((rhs, rim), F32), ((rhs, rim), F32)],
        [pltpu.VMEM(panels.shape, F32), pltpu.VMEM(leaf_order.shape, jnp.int32), dma((2,))],
        MIB0,
    )
    across = [(i, i + 1) for i in range(1, devices - 1, 2)]
    far_rim = lax.ppermute(far_rim, "leaf", across + [(j, i) for i, j in across])
    pairs, packet, inverse = call(
        up_kernel,
        "vvvhh",
        (middle, near_rim, leaf_order, leaf_basis, mats),
        [
            ((leaves // 2 - 1, rhs, 2 * rank), F32),
            ((rhs, rim + 2 * rank), F32),
            ((leaves, size), jnp.int32),
        ],
        [basis_shape, mats_shape, dma((CHUNKS,)), dma((MCHUNKS,))],
    )
    if EARLY:
        packet, far_rim = lax.optimization_barrier((packet, far_rim))
    other = lax.ppermute(packet, "leaf", [(i, i ^ 1) for i in range(devices)])
    chips = devices // 2
    own, packets = call(
        join_kernel,
        "vvvv",
        (middle, packet, other, far_rim),
        [((rhs, length), F32), ((chips, rhs // 2, 2 * rank), F32)],
        alias={0: 0},
    )
    others = [turned(own, k) for k in (1, 2, 3)]
    groups = [[core + 2 * i for i in range(chips)] for core in (0, 1)]
    gathered = lax.all_to_all(packets, "leaf", 0, 0, axis_index_groups=groups)

    near = call(
        near_kernel,
        "svvvvh",
        (near_cols.T, own, *others, near_tiles),
        [((rhs, leaves * near_tiles.shape[2]), F32)] * 4,
        [
            pltpu.VMEM((leaves + 2 * W, 2 * parts * rhs, size), BF16),
            pltpu.VMEM(near_tiles.shape, F32),
            dma((4,)),
        ],
        0,
        NEAR_US,
    )
    back = [near[0]] + [turned(near[k], -k) for k in (1, 2, 3)]

    (far,) = call(
        down_kernel,
        "ssvvvhhhh",
        (cross_flags, local_flags, gathered, other, pairs, leaf_basis, mats, cross_coupling, cross_transfer),
        [((rhs, leaves * size), F32)],
        [
            pltpu.VMEM((devices - 2, rhs, rank), F32),
            basis_shape,
            mats_shape,
            pltpu.VMEM((devices.bit_length() - 2, rank, rank), F32),
            pltpu.VMEM(cross_transfer.shape, F32),
            dma((devices.bit_length() + 2,)),
        ],
    )
    (out,) = call(
        final_kernel,
        "vvvvvv",
        (inverse, far, *back),
        [((rhs, leaves * size), F32)],
        [pltpu.VMEM(panels.shape, F32), dma((4,))],
        out_space=hbm,
    )
    return out


def solution(mesh):
    return jax.shard_map(
        local,
        mesh=mesh,
        in_specs=(
            P("vec", "leaf"),
            P("leaf", None, "vec", None),
            P("leaf", None),
            P("leaf", None),
            P("leaf", None, None),
            P("leaf", None, None, None),
            P("leaf", None),
            P(),
            P(),
            P(),
        ),
        out_specs=P("vec", "leaf"),
        check_vma=False,
    )
```

```python
import math

import jax
import jax.numpy as jnp
from jax import lax
from jax.experimental import pallas as pl
from jax.experimental.pallas import tpu as pltpu
from jax.sharding import PartitionSpec as P

W = 8
NEAR_US = 5
TIE = 1
PATH_US = 0
CHUNKS = 2
UNROLL = 4
MIB = 52
MIB0 = 52
ROOT_HALF = 1.0 / math.sqrt(2.0)
F32, BF16 = jnp.float32, jnp.bfloat16
NN = (((1,), (0,)), ((), ()))
NT = (((1,), (1,)), ((), ()))


def params(mib):
    return pltpu.CompilerParams(vmem_limit_bytes=int(mib * 1024 * 1024))


def vmem():
    return pl.BlockSpec(memory_space=pltpu.VMEM)


def smem():
    return pl.BlockSpec(memory_space=pltpu.SMEM)


def hbm():
    return pl.BlockSpec(memory_space=pltpu.HBM)


def halves(x):
    hi = x.astype(BF16).astype(F32)
    return hi, x - hi


def left_rows(x):
    hi, lo = halves(x)
    rows = jnp.concatenate([hi, lo], axis=0).astype(BF16)
    return jnp.concatenate([rows, rows], axis=1)


def mul_nn(x, w):
    m = x.shape[0]
    hi, lo = halves(w)
    both = jnp.concatenate([hi.astype(BF16), lo.astype(BF16)], axis=0)
    d = lax.dot_general(left_rows(x), both, NN, preferred_element_type=F32)
    return d[:m] + d[m:]


def mul_nt(x, w):
    m = x.shape[0]
    hi, lo = halves(w)
    both = jnp.concatenate([hi.astype(BF16), lo.astype(BF16)], axis=1)
    d = lax.dot_general(left_rows(x), both, NT, preferred_element_type=F32)
    return d[:m] + d[m:]


def lane_gather(x, index):
    return jnp.take_along_axis(x, index, axis=1, mode="promise_in_bounds")


def invert(order, inverse):
    leaves = order.shape[0]
    rows = lax.broadcasted_iota(jnp.int32, (128, 128), 0)
    places = lax.broadcasted_iota(jnp.int32, (16, 128), 1).astype(F32).astype(BF16)
    for i in range(leaves):
        hot = (jnp.broadcast_to(order[i : i + 1, :], (128, 128)) == rows).astype(F32).astype(BF16)
        inv = lax.dot_general(places, hot, NT, preferred_element_type=F32)
        inverse[i : i + 1, :] = inv[0:1].astype(jnp.int32)


def up_kernel(
    panels_hbm, order_hbm, basis_hbm, mats_hbm, middle, far_rim, pairs, packet, inverse,
    panels, order, basis, mats, sems, basis_sems, mats_sems,
):
    copies = [
        pltpu.make_async_copy(order_hbm, order, sems.at[0]),
        pltpu.make_async_copy(panels_hbm, panels, sems.at[1]),
    ]
    for copy in copies:
        copy.start()
    leaves = basis.shape[0]
    rank = basis.shape[1]
    count = leaves // 2
    chunks = basis_sems.shape[0]
    basis_copies = chunked(basis_hbm, basis, basis_sems, chunks)
    mats_copies = chunked(mats_hbm, mats, mats_sems, mats_sems.shape[0])
    even = (lax.axis_index("leaf") & 1) == 0
    for copy in copies:
        copy.wait()
    for i in range(leaves):
        index = jnp.broadcast_to(order[i : i + 1, :], (panels.shape[0], 128))
        placed = lane_gather(panels[:, 128 * i : 128 * (i + 1)], index)
        middle[:, 128 * (i + W) : 128 * (i + W + 1)] = placed
    for i in range(W):
        first = middle[:, 128 * (i + W) : 128 * (i + W + 1)]
        last = middle[:, 128 * (i + leaves) : 128 * (i + leaves + 1)]
        at = slice(128 * i, 128 * (i + 1))
        packet[:, at] = jnp.where(even, last, first)
        far_rim[:, at] = jnp.where(even, first, last)
    invert(order, inverse)
    nodes = []
    for j in range(0, count, 2):
        if j % (count // chunks) == 0:
            basis_copies[j // (count // chunks)].wait()
        at = 128 * (2 * j + W)
        x = jnp.concatenate([middle[:, at : at + 256], middle[:, at + 256 : at + 512]], axis=0)
        w = jnp.concatenate(
            [
                jnp.concatenate([basis[2 * j], basis[2 * j + 1]], axis=1),
                jnp.concatenate([basis[2 * j + 2], basis[2 * j + 3]], axis=1),
            ],
            axis=0,
        )
        both = mul_nt(x, w) * ROOT_HALF
        half = both.shape[0] // 2
        nodes += [both[:half, :rank], both[half:, rank:]]
    first_pair, first_node = 0, 0
    for copy in mats_copies:
        copy.wait()
    while count > 1:
        lifted = []
        for j in range(count // 2):
            pair = jnp.concatenate([nodes[2 * j], nodes[2 * j + 1]], axis=1)
            pairs[first_pair + j] = pair
            at = first_node + 2 * j
            w = mats[at : at + 2].reshape(2 * rank, 2 * rank)
            lifted.append(mul_nn(pair, w)[:, rank:] * ROOT_HALF)
        nodes = lifted
        first_pair += count // 2
        first_node += count
        count //= 2
    skel = nodes[0]
    lift = mul_nn(skel, mats[first_node])[:, rank:]
    packet[:, far_rim.shape[1] :] = jnp.concatenate([skel, lift], axis=1)


def path_kernel(
    after, mats_hbm, coupling_hbm, transfer_hbm, path, own, coupling, transfer, sems
):
    del after
    me = lax.axis_index("leaf")
    levels = coupling.shape[0]
    rank = own.shape[0]
    copies = [pltpu.make_async_copy(mats_hbm.at[mats_hbm.shape[0] - 1], own, sems.at[0])]
    for c in range(1, levels + 1):
        node = (2 << levels) - (2 << levels >> (c - 1)) + (me >> c)
        copies.append(pltpu.make_async_copy(coupling_hbm.at[node], coupling.at[c - 1], sems.at[2 * c - 1]))
        if c < levels:
            copies.append(pltpu.make_async_copy(transfer_hbm.at[node], transfer.at[c - 1], sems.at[2 * c]))
    for copy in copies:
        copy.start()
    for copy in copies:
        copy.wait()
    down = own[:, rank:]
    terms = [own[:, :rank]]
    for c in range(levels):
        terms.append(mul_nn(down, coupling[c]))
        if c < levels - 1:
            down = mul_nn(down, transfer[c])
    for i in range(len(terms) // 2):
        path[i] = jnp.concatenate([terms[2 * i], terms[2 * i + 1]], axis=1)


def join_kernel(middle, packet, other, far_rim, extended, packets):
    del middle
    even = (lax.axis_index("leaf") & 1) == 0
    width = far_rim.shape[1]
    near_rim = other[:, :width]
    extended[:, :width] = jnp.where(even, far_rim[...], near_rim)
    extended[:, extended.shape[1] - width :] = jnp.where(even, near_rim, far_rim[...])
    half = packets.shape[1]
    rank = packets.shape[2] // 2
    lift = width + rank
    node = (packet[:, lift:] + other[:, lift:]) * ROOT_HALF
    rows = jnp.concatenate([node[:half], node[half:]], axis=1)
    packets[...] = jnp.broadcast_to(rows[None], packets.shape)


def near_kernel(cols, own, arr1, arr2, arr3, tiles_hbm, out0, out1, out2, out3, held, tiles, sems):
    copies = chunked(tiles_hbm, tiles, sems, 4)
    leaves = tiles.shape[0]
    slots = tiles.shape[1]
    base = lax.axis_index("leaf") * leaves - W
    outs = (out0, out1, out2, out3)

    def hold(i, carry):
        at = pl.ds(pl.multiple_of(i * 128, 128), 128)
        x = jnp.concatenate([ref[:, at] for ref in (own, arr1, arr2, arr3)], axis=0)
        hi, lo = halves(x)
        held[i] = jnp.concatenate([hi.astype(BF16), lo.astype(BF16)], axis=0)
        return carry

    lax.fori_loop(0, leaves + 2 * W, hold, 0, unroll=8)

    def group(g, carry):
        parts = []
        for k in range(4):
            i = 4 * g + k
            x = jnp.concatenate([held[cols[n, i] - base] for n in range(slots)], axis=1)
            t = jnp.concatenate([tiles[i, n] for n in range(slots)], axis=1)
            hi, lo = halves(t)
            w = jnp.concatenate([hi.astype(BF16), lo.astype(BF16)], axis=0)
            d = lax.dot_general(x, w, NT, preferred_element_type=F32)
            m, q = d.shape[0] // 2, d.shape[1] // 2
            parts.append(d[:m, :q] + (d[:m, q:] + d[m:, :q]))
        rows = jnp.concatenate(parts, axis=1)
        at = pl.ds(pl.multiple_of(g * 128, 128), 128)
        for k in range(4):
            outs[k][:, at] = rows[8 * k : 8 * (k + 1)]
        return carry

    quarter = leaves // 16
    for c in range(4):
        copies[c].wait()
        lax.fori_loop(c * quarter, (c + 1) * quarter, group, 0, unroll=UNROLL)


def down_kernel(
    cross_flags, flags, packets, other, pairs, path, basis_hbm, mats_hbm, transfer_hbm,
    far, skels, basis, mats, transfer, sems,
):
    leaves = basis.shape[0]
    rank = basis.shape[1]
    devices = 2 * packets.shape[0]
    depth = devices.bit_length() - 1
    me = lax.axis_index("leaf")
    skel = other.shape[1] - 2 * rank
    transfer_copy = pltpu.make_async_copy(transfer_hbm, transfer, sems.at[0])
    transfer_copy.start()
    mats_copy = pltpu.make_async_copy(mats_hbm, mats, sems.at[1])
    mats_copy.start()
    basis_copy = pltpu.make_async_copy(basis_hbm, basis, sems.at[2])
    basis_copy.start()
    count = devices // 2
    nodes = [
        jnp.concatenate([packets[j][:, :rank], packets[j][:, rank:]], axis=0) for j in range(count)
    ]
    first = 0
    transfer_copy.wait()
    while count > 1:
        for j in range(count):
            skels[first + j] = nodes[j]
        if count > 2:
            lifted = []
            for j in range(count // 2):
                pair = jnp.concatenate([nodes[2 * j], nodes[2 * j + 1]], axis=1)
                at = first + 2 * j
                w = transfer[at : at + 2].reshape(2 * rank, rank)
                lifted.append(mul_nn(pair, w) * ROOT_HALF)
            nodes = lifted
        first += count
        count //= 2
    top = leaves - 2
    terms = [other[:, skel : skel + rank] * flags[0, top].astype(F32)]
    for c in range(1, depth):
        start = devices - (devices >> (c - 1))
        node = start + (me >> c)
        sibling = start + ((me >> c) ^ 1)
        terms.append(skels[sibling] * cross_flags[node].astype(F32))
    z = None
    for i in range(len(terms) // 2):
        part = mul_nt(jnp.concatenate([terms[2 * i], terms[2 * i + 1]], axis=1), path[i])
        z = part if z is None else z + part
    zs = [z]
    mats_copy.wait()
    count = 2
    while count < leaves:
        first_node = leaves - 2 * count
        first_pair = (leaves - 2 * count) // 2
        lower = []
        for j in range(count // 2):
            pair = pairs[first_pair + j]
            z = zs[j]
            node = first_node + 2 * j
            left = jnp.concatenate([pair[:, rank:] * flags[0, node].astype(F32), z], axis=1)
            right = jnp.concatenate([pair[:, :rank] * flags[0, node + 1].astype(F32), z], axis=1)
            w = mats[node : node + 2].reshape(2 * rank, 2 * rank)
            both = mul_nt(jnp.concatenate([left, right], axis=0), w)
            half = both.shape[0] // 2
            lower += [both[:half, :rank], both[half:, rank:]]
        zs = lower
        count *= 2
    basis_copy.wait()
    for j in range(leaves // 2):
        w = jnp.concatenate([basis[2 * j], basis[2 * j + 1]], axis=1)
        both = mul_nn(zs[j], w)
        far[:, 256 * j : 256 * (j + 1)] = both


def final_kernel(inverse, far, near0, near1, near2, near3, out_hbm, out, sems):
    leaves = inverse.shape[0]
    me = lax.axis_index("vec")
    nears = (near0, near1, near2, near3)
    copies = []
    chunk = leaves // sems.shape[0]
    for i in range(leaves):
        index = jnp.broadcast_to(inverse[i : i + 1, :], (out.shape[0], 128))
        owner = ((index >> 5) - me) & 3
        place = (index & 31) + 32 * (i % 4)
        at = slice(128 * (i // 4), 128 * (i // 4 + 1))
        near = lane_gather(near0[:, at], place)
        for k in (1, 2, 3):
            near = jnp.where(owner == k, lane_gather(nears[k][:, at], place), near)
        spot = slice(128 * i, 128 * (i + 1))
        out[:, spot] = near + lane_gather(far[:, spot], index)
        if (i + 1) % chunk == 0:
            c = i // chunk
            at = pl.ds(128 * chunk * c, 128 * chunk)
            copies.append(pltpu.make_async_copy(out.at[:, at], out_hbm.at[:, at], sems.at[c]))
            copies[-1].start()
    for copy in copies:
        copy.wait()


def call(kernel, spaces, ins, out_shapes, scratch=(), mib=0, us=0, out_space=vmem, alias={}):
    place = {"s": smem, "v": vmem, "h": hbm}
    return pl.pallas_call(
        kernel,
        out_shape=[jax.ShapeDtypeStruct(s, t) for s, t in out_shapes],
        in_specs=[place[k]() for k in spaces],
        out_specs=[out_space()] * len(out_shapes),
        scratch_shapes=list(scratch),
        input_output_aliases=alias,
        compiler_params=params(mib or MIB),
        cost_estimate=pl.CostEstimate(flops=int(us * 1.15e9), bytes_accessed=0, transcendentals=0) if us else None,
    )(*ins)


def chunked(source, target, sems, chunks):
    step = -(-source.shape[0] // chunks)
    copies = []
    for c in range(chunks):
        at = pl.ds(c * step, min(step, source.shape[0] - c * step))
        copies.append(pltpu.make_async_copy(source.at[at], target.at[at], sems.at[c]))
        copies[-1].start()
    return copies


def local(
    panels,
    near_tiles,
    near_cols,
    leaf_order,
    leaf_basis,
    local_mats,
    local_flags,
    cross_coupling,
    cross_transfer,
    cross_flags,
):
    rhs = panels.shape[0]
    leaves, rank, size = leaf_basis.shape
    devices = lax.axis_size("leaf")
    parts = lax.axis_size("vec")
    mats = local_mats[0]
    rim = W * size

    def turned(x, k):
        return lax.ppermute(x, "vec", [(i, (i + k) % parts) for i in range(parts)])

    dma = pltpu.SemaphoreType.DMA

    basis_shape = pltpu.VMEM(leaf_basis.shape, F32)
    mats_shape = pltpu.VMEM(mats.shape, F32)
    length = (leaves + 2 * W) * size
    levels = devices.bit_length() - 2
    middle, far_rim, pairs, packet, inverse = call(
        up_kernel,
        "hhhh",
        (panels, leaf_order, leaf_basis, mats),
        [
            ((rhs, length), F32),
            ((rhs, rim), F32),
            ((leaves // 2 - 1, rhs, 2 * rank), F32),
            ((rhs, rim + 2 * rank), F32),
            ((leaves, size), jnp.int32),
        ],
        [
            pltpu.VMEM(panels.shape, F32),
            pltpu.VMEM(leaf_order.shape, jnp.int32),
            basis_shape,
            mats_shape,
            dma((2,)),
            dma((CHUNKS,)),
            dma((1,)),
        ],
        MIB0,
    )
    across = [(i, i + 1) for i in range(1, devices - 1, 2)]
    far_rim = lax.ppermute(far_rim, "leaf", across + [(j, i) for i, j in across])
    other = lax.ppermute(packet, "leaf", [(i, i ^ 1) for i in range(devices)])
    chips = devices // 2
    own, packets = call(
        join_kernel,
        "vvvv",
        (middle, packet, other, far_rim),
        [((rhs, length), F32), ((chips, rhs // 2, 2 * rank), F32)],
        alias={0: 0},
    )
    others = [turned(own, k) for k in (1, 2, 3)]
    groups = [[core + 2 * i for i in range(chips)] for core in (0, 1)]
    gathered = lax.all_to_all(packets, "leaf", 0, 0, axis_index_groups=groups)

    (path,) = call(
        path_kernel,
        "vhhh",
        (other, mats, cross_coupling, cross_transfer),
        [(((levels + 1) // 2, rank, 2 * rank), F32)],
        [
            pltpu.VMEM(mats.shape[1:], F32),
            pltpu.VMEM((levels, rank, rank), F32),
            pltpu.VMEM((levels - 1, rank, rank), F32),
            dma((2 * levels,)),
        ],
        us=PATH_US,
    )
    cols = near_cols.T
    if TIE:
        cols, path = lax.optimization_barrier((cols, path))
    near = call(
        near_kernel,
        "svvvvh",
        (cols, own, *others, near_tiles),
        [((rhs, leaves * near_tiles.shape[2]), F32)] * 4,
        [
            pltpu.VMEM((leaves + 2 * W, 2 * parts * rhs, size), BF16),
            pltpu.VMEM(near_tiles.shape, F32),
            dma((4,)),
        ],
        0,
        NEAR_US,
    )
    back = [near[0]] + [turned(near[k], -k) for k in (1, 2, 3)]

    (far,) = call(
        down_kernel,
        "ssvvvvhhh",
        (cross_flags, local_flags, gathered, other, pairs, path, leaf_basis, mats, cross_transfer),
        [((rhs, leaves * size), F32)],
        [
            pltpu.VMEM((devices - 2, rhs, rank), F32),
            basis_shape,
            mats_shape,
            pltpu.VMEM(cross_transfer.shape, F32),
            dma((3,)),
        ],
    )
    (out,) = call(
        final_kernel,
        "vvvvvv",
        (inverse, far, *back),
        [((rhs, leaves * size), F32)],
        [pltpu.VMEM(panels.shape, F32), dma((4,))],
        out_space=hbm,
    )
    return out


def solution(mesh):
    return jax.shard_map(
        local,
        mesh=mesh,
        in_specs=(
            P("vec", "leaf"),
            P("leaf", None, "vec", None),
            P("leaf", None),
            P("leaf", None),
            P("leaf", None, None),
            P("leaf", None, None, None),
            P("leaf", None),
            P(),
            P(),
            P(),
        ),
        out_specs=P("vec", "leaf"),
        check_vma=False,
    )
```

```python
import math

import jax
import jax.numpy as jnp
from jax import lax
from jax.experimental import pallas as pl
from jax.experimental.pallas import tpu as pltpu
from jax.sharding import PartitionSpec as P

W = 8
NEAR_US = 5
TIE = 1
PATH_US = 0
CHUNKS = 2
UNROLL = 4
MIB = 52
MIB0 = 52
ROOT_HALF = 1.0 / math.sqrt(2.0)
F32, BF16 = jnp.float32, jnp.bfloat16
NN = (((1,), (0,)), ((), ()))
NT = (((1,), (1,)), ((), ()))


def params(mib):
    return pltpu.CompilerParams(vmem_limit_bytes=int(mib * 1024 * 1024))


def vmem():
    return pl.BlockSpec(memory_space=pltpu.VMEM)


def smem():
    return pl.BlockSpec(memory_space=pltpu.SMEM)


def hbm():
    return pl.BlockSpec(memory_space=pltpu.HBM)


def halves(x):
    hi = x.astype(BF16).astype(F32)
    return hi, x - hi


def left_rows(x):
    hi, lo = halves(x)
    rows = jnp.concatenate([hi, lo], axis=0).astype(BF16)
    return jnp.concatenate([rows, rows], axis=1)


def mul_nn(x, w):
    m = x.shape[0]
    hi, lo = halves(w)
    both = jnp.concatenate([hi.astype(BF16), lo.astype(BF16)], axis=0)
    d = lax.dot_general(left_rows(x), both, NN, preferred_element_type=F32)
    return d[:m] + d[m:]


def mul_nt(x, w):
    m = x.shape[0]
    hi, lo = halves(w)
    both = jnp.concatenate([hi.astype(BF16), lo.astype(BF16)], axis=1)
    d = lax.dot_general(left_rows(x), both, NT, preferred_element_type=F32)
    return d[:m] + d[m:]


def lane_gather(x, index):
    return jnp.take_along_axis(x, index, axis=1, mode="promise_in_bounds")


def invert(order, inverse):
    leaves = order.shape[0]
    rows = lax.broadcasted_iota(jnp.int32, (128, 128), 0)
    places = lax.broadcasted_iota(jnp.int32, (16, 128), 1).astype(F32).astype(BF16)
    for i in range(leaves):
        hot = (jnp.broadcast_to(order[i : i + 1, :], (128, 128)) == rows).astype(F32).astype(BF16)
        inv = lax.dot_general(places, hot, NT, preferred_element_type=F32)
        inverse[i : i + 1, :] = inv[0:1].astype(jnp.int32)


def up_kernel(
    panels_hbm, order_hbm, basis_hbm, mats_hbm, middle, far_rim, pairs, packet, inverse,
    panels, order, basis, mats, sems, basis_sems, mats_sems,
):
    copies = [
        pltpu.make_async_copy(order_hbm, order, sems.at[0]),
        pltpu.make_async_copy(panels_hbm, panels, sems.at[1]),
    ]
    for copy in copies:
        copy.start()
    leaves = basis.shape[0]
    rank = basis.shape[1]
    count = leaves // 2
    chunks = basis_sems.shape[0]
    basis_copies = chunked(basis_hbm, basis, basis_sems, chunks)
    mats_copies = chunked(mats_hbm, mats, mats_sems, mats_sems.shape[0])
    even = (lax.axis_index("leaf") & 1) == 0
    for copy in copies:
        copy.wait()
    for i in range(leaves):
        index = jnp.broadcast_to(order[i : i + 1, :], (panels.shape[0], 128))
        placed = lane_gather(panels[:, 128 * i : 128 * (i + 1)], index)
        middle[:, 128 * (i + W) : 128 * (i + W + 1)] = placed
    for i in range(W):
        first = middle[:, 128 * (i + W) : 128 * (i + W + 1)]
        last = middle[:, 128 * (i + leaves) : 128 * (i + leaves + 1)]
        at = slice(128 * i, 128 * (i + 1))
        packet[:, at] = jnp.where(even, last, first)
        far_rim[:, at] = jnp.where(even, first, last)
    invert(order, inverse)
    nodes = []
    for j in range(0, count, 2):
        if j % (count // chunks) == 0:
            basis_copies[j // (count // chunks)].wait()
        at = 128 * (2 * j + W)
        x = jnp.concatenate([middle[:, at : at + 256], middle[:, at + 256 : at + 512]], axis=0)
        w = jnp.concatenate(
            [
                jnp.concatenate([basis[2 * j], basis[2 * j + 1]], axis=1),
                jnp.concatenate([basis[2 * j + 2], basis[2 * j + 3]], axis=1),
            ],
            axis=0,
        )
        both = mul_nt(x, w) * ROOT_HALF
        half = both.shape[0] // 2
        nodes += [both[:half, :rank], both[half:, rank:]]
    first_pair, first_node = 0, 0
    for copy in mats_copies:
        copy.wait()
    while count > 1:
        lifted = []
        for j in range(count // 2):
            pair = jnp.concatenate([nodes[2 * j], nodes[2 * j + 1]], axis=1)
            pairs[first_pair + j] = pair
            at = first_node + 2 * j
            w = mats[at : at + 2].reshape(2 * rank, 2 * rank)
            lifted.append(mul_nn(pair, w)[:, rank:] * ROOT_HALF)
        nodes = lifted
        first_pair += count // 2
        first_node += count
        count //= 2
    skel = nodes[0]
    lift = mul_nn(skel, mats[first_node])[:, rank:]
    packet[:, far_rim.shape[1] :] = jnp.concatenate([skel, lift], axis=1)


def path_kernel(
    after, mats_hbm, coupling_hbm, transfer_hbm, path, own, coupling, transfer, sems
):
    del after
    me = lax.axis_index("leaf")
    levels = coupling.shape[0]
    rank = own.shape[0]
    copies = [pltpu.make_async_copy(mats_hbm.at[mats_hbm.shape[0] - 1], own, sems.at[0])]
    for c in range(1, levels + 1):
        node = (2 << levels) - (2 << levels >> (c - 1)) + (me >> c)
        copies.append(pltpu.make_async_copy(coupling_hbm.at[node], coupling.at[c - 1], sems.at[2 * c - 1]))
        if c < levels:
            copies.append(pltpu.make_async_copy(transfer_hbm.at[node], transfer.at[c - 1], sems.at[2 * c]))
    for copy in copies:
        copy.start()
    for copy in copies:
        copy.wait()
    down = own[:, rank:]
    terms = [own[:, :rank]]
    for c in range(levels):
        terms.append(mul_nn(down, coupling[c]))
        if c < levels - 1:
            down = mul_nn(down, transfer[c])
    for i in range(len(terms) // 2):
        path[i] = jnp.concatenate([terms[2 * i], terms[2 * i + 1]], axis=1)


def join_kernel(middle, packet, other, far_rim, extended, packets):
    del middle
    even = (lax.axis_index("leaf") & 1) == 0
    width = far_rim.shape[1]
    near_rim = other[:, :width]
    extended[:, :width] = jnp.where(even, far_rim[...], near_rim)
    extended[:, extended.shape[1] - width :] = jnp.where(even, near_rim, far_rim[...])
    half = packets.shape[1]
    rank = packets.shape[2] // 2
    lift = width + rank
    node = (packet[:, lift:] + other[:, lift:]) * ROOT_HALF
    rows = jnp.concatenate([node[:half], node[half:]], axis=1)
    packets[...] = jnp.broadcast_to(rows[None], packets.shape)


def near_kernel(cols, own, arr1, arr2, arr3, tiles, out0, out1, out2, out3, held):
    leaves = tiles.shape[0]
    slots = tiles.shape[1]
    base = lax.axis_index("leaf") * leaves - W
    outs = (out0, out1, out2, out3)

    def hold(i, carry):
        at = pl.ds(pl.multiple_of(i * 128, 128), 128)
        x = jnp.concatenate([ref[:, at] for ref in (own, arr1, arr2, arr3)], axis=0)
        hi, lo = halves(x)
        held[i] = jnp.concatenate([hi.astype(BF16), lo.astype(BF16)], axis=0)
        return carry

    lax.fori_loop(0, leaves + 2 * W, hold, 0, unroll=8)

    def group(g, carry):
        parts = []
        for k in range(4):
            i = 4 * g + k
            x = jnp.concatenate([held[cols[n, i] - base] for n in range(slots)], axis=1)
            t = jnp.concatenate([tiles[i, n] for n in range(slots)], axis=1)
            hi, lo = halves(t)
            w = jnp.concatenate([hi.astype(BF16), lo.astype(BF16)], axis=0)
            d = lax.dot_general(x, w, NT, preferred_element_type=F32)
            m, q = d.shape[0] // 2, d.shape[1] // 2
            parts.append(d[:m, :q] + (d[:m, q:] + d[m:, :q]))
        rows = jnp.concatenate(parts, axis=1)
        at = pl.ds(pl.multiple_of(g * 128, 128), 128)
        for k in range(4):
            outs[k][:, at] = rows[8 * k : 8 * (k + 1)]
        return carry

    quarter = leaves // 16
    for c in range(4):
        lax.fori_loop(c * quarter, (c + 1) * quarter, group, 0, unroll=UNROLL)


def down_kernel(
    cross_flags, flags, packets, other, pairs, path, basis_hbm, mats_hbm, transfer_hbm,
    far, skels, basis, mats, transfer, sems,
):
    leaves = basis.shape[0]
    rank = basis.shape[1]
    devices = 2 * packets.shape[0]
    depth = devices.bit_length() - 1
    me = lax.axis_index("leaf")
    skel = other.shape[1] - 2 * rank
    transfer_copy = pltpu.make_async_copy(transfer_hbm, transfer, sems.at[0])
    transfer_copy.start()
    mats_copy = pltpu.make_async_copy(mats_hbm, mats, sems.at[1])
    mats_copy.start()
    basis_copy = pltpu.make_async_copy(basis_hbm, basis, sems.at[2])
    basis_copy.start()
    count = devices // 2
    nodes = [
        jnp.concatenate([packets[j][:, :rank], packets[j][:, rank:]], axis=0) for j in range(count)
    ]
    first = 0
    transfer_copy.wait()
    while count > 1:
        for j in range(count):
            skels[first + j] = nodes[j]
        if count > 2:
            lifted = []
            for j in range(count // 2):
                pair = jnp.concatenate([nodes[2 * j], nodes[2 * j + 1]], axis=1)
                at = first + 2 * j
                w = transfer[at : at + 2].reshape(2 * rank, rank)
                lifted.append(mul_nn(pair, w) * ROOT_HALF)
            nodes = lifted
        first += count
        count //= 2
    top = leaves - 2
    terms = [other[:, skel : skel + rank] * flags[0, top].astype(F32)]
    for c in range(1, depth):
        start = devices - (devices >> (c - 1))
        node = start + (me >> c)
        sibling = start + ((me >> c) ^ 1)
        terms.append(skels[sibling] * cross_flags[node].astype(F32))
    z = None
    for i in range(len(terms) // 2):
        part = mul_nt(jnp.concatenate([terms[2 * i], terms[2 * i + 1]], axis=1), path[i])
        z = part if z is None else z + part
    zs = [z]
    mats_copy.wait()
    count = 2
    while count < leaves:
        first_node = leaves - 2 * count
        first_pair = (leaves - 2 * count) // 2
        lower = []
        for j in range(count // 2):
            pair = pairs[first_pair + j]
            z = zs[j]
            node = first_node + 2 * j
            left = jnp.concatenate([pair[:, rank:] * flags[0, node].astype(F32), z], axis=1)
            right = jnp.concatenate([pair[:, :rank] * flags[0, node + 1].astype(F32), z], axis=1)
            w = mats[node : node + 2].reshape(2 * rank, 2 * rank)
            both = mul_nt(jnp.concatenate([left, right], axis=0), w)
            half = both.shape[0] // 2
            lower += [both[:half, :rank], both[half:, rank:]]
        zs = lower
        count *= 2
    basis_copy.wait()
    for j in range(leaves // 2):
        w = jnp.concatenate([basis[2 * j], basis[2 * j + 1]], axis=1)
        both = mul_nn(zs[j], w)
        far[:, 256 * j : 256 * (j + 1)] = both


def final_kernel(inverse, far, near0, near1, near2, near3, out_hbm, out, sems):
    leaves = inverse.shape[0]
    me = lax.axis_index("vec")
    nears = (near0, near1, near2, near3)
    copies = []
    chunk = leaves // sems.shape[0]
    for i in range(leaves):
        index = jnp.broadcast_to(inverse[i : i + 1, :], (out.shape[0], 128))
        owner = ((index >> 5) - me) & 3
        place = (index & 31) + 32 * (i % 4)
        at = slice(128 * (i // 4), 128 * (i // 4 + 1))
        near = lane_gather(near0[:, at], place)
        for k in (1, 2, 3):
            near = jnp.where(owner == k, lane_gather(nears[k][:, at], place), near)
        spot = slice(128 * i, 128 * (i + 1))
        out[:, spot] = near + lane_gather(far[:, spot], index)
        if (i + 1) % chunk == 0:
            c = i // chunk
            at = pl.ds(128 * chunk * c, 128 * chunk)
            copies.append(pltpu.make_async_copy(out.at[:, at], out_hbm.at[:, at], sems.at[c]))
            copies[-1].start()
    for copy in copies:
        copy.wait()


def call(kernel, spaces, ins, out_shapes, scratch=(), mib=0, us=0, out_space=vmem, alias={}):
    place = {"s": smem, "v": vmem, "h": hbm}
    return pl.pallas_call(
        kernel,
        out_shape=[jax.ShapeDtypeStruct(s, t) for s, t in out_shapes],
        in_specs=[place[k]() for k in spaces],
        out_specs=[out_space()] * len(out_shapes),
        scratch_shapes=list(scratch),
        input_output_aliases=alias,
        compiler_params=params(mib or MIB),
        cost_estimate=pl.CostEstimate(flops=int(us * 1.15e9), bytes_accessed=0, transcendentals=0) if us else None,
    )(*ins)


def chunked(source, target, sems, chunks):
    step = -(-source.shape[0] // chunks)
    copies = []
    for c in range(chunks):
        at = pl.ds(c * step, min(step, source.shape[0] - c * step))
        copies.append(pltpu.make_async_copy(source.at[at], target.at[at], sems.at[c]))
        copies[-1].start()
    return copies


def local(
    panels,
    near_tiles,
    near_cols,
    leaf_order,
    leaf_basis,
    local_mats,
    local_flags,
    cross_coupling,
    cross_transfer,
    cross_flags,
):
    rhs = panels.shape[0]
    leaves, rank, size = leaf_basis.shape
    devices = lax.axis_size("leaf")
    parts = lax.axis_size("vec")
    mats = local_mats[0]
    rim = W * size

    def turned(x, k):
        return lax.ppermute(x, "vec", [(i, (i + k) % parts) for i in range(parts)])

    dma = pltpu.SemaphoreType.DMA

    basis_shape = pltpu.VMEM(leaf_basis.shape, F32)
    mats_shape = pltpu.VMEM(mats.shape, F32)
    length = (leaves + 2 * W) * size
    levels = devices.bit_length() - 2
    middle, far_rim, pairs, packet, inverse = call(
        up_kernel,
        "hhhh",
        (panels, leaf_order, leaf_basis, mats),
        [
            ((rhs, length), F32),
            ((rhs, rim), F32),
            ((leaves // 2 - 1, rhs, 2 * rank), F32),
            ((rhs, rim + 2 * rank), F32),
            ((leaves, size), jnp.int32),
        ],
        [
            pltpu.VMEM(panels.shape, F32),
            pltpu.VMEM(leaf_order.shape, jnp.int32),
            basis_shape,
            mats_shape,
            dma((2,)),
            dma((CHUNKS,)),
            dma((1,)),
        ],
        MIB0,
    )
    across = [(i, i + 1) for i in range(1, devices - 1, 2)]
    far_rim = lax.ppermute(far_rim, "leaf", across + [(j, i) for i, j in across])
    other = lax.ppermute(packet, "leaf", [(i, i ^ 1) for i in range(devices)])
    chips = devices // 2
    own, packets = call(
        join_kernel,
        "vvvv",
        (middle, packet, other, far_rim),
        [((rhs, length), F32), ((chips, rhs // 2, 2 * rank), F32)],
        alias={0: 0},
    )
    others = [turned(own, k) for k in (1, 2, 3)]
    groups = [[core + 2 * i for i in range(chips)] for core in (0, 1)]
    gathered = lax.all_to_all(packets, "leaf", 0, 0, axis_index_groups=groups)

    (path,) = call(
        path_kernel,
        "vhhh",
        (other, mats, cross_coupling, cross_transfer),
        [(((levels + 1) // 2, rank, 2 * rank), F32)],
        [
            pltpu.VMEM(mats.shape[1:], F32),
            pltpu.VMEM((levels, rank, rank), F32),
            pltpu.VMEM((levels - 1, rank, rank), F32),
            dma((2 * levels,)),
        ],
        us=PATH_US,
    )
    cols = near_cols.T
    if TIE:
        cols, path = lax.optimization_barrier((cols, path))
    near = call(
        near_kernel,
        "svvvvv",
        (cols, own, *others, near_tiles),
        [((rhs, leaves * near_tiles.shape[2]), F32)] * 4,
        [
            pltpu.VMEM((leaves + 2 * W, 2 * parts * rhs, size), BF16),
        ],
        46,
        NEAR_US,
    )
    back = [near[0]] + [turned(near[k], -k) for k in (1, 2, 3)]

    (far,) = call(
        down_kernel,
        "ssvvvvhhh",
        (cross_flags, local_flags, gathered, other, pairs, path, leaf_basis, mats, cross_transfer),
        [((rhs, leaves * size), F32)],
        [
            pltpu.VMEM((devices - 2, rhs, rank), F32),
            basis_shape,
            mats_shape,
            pltpu.VMEM(cross_transfer.shape, F32),
            dma((3,)),
        ],
    )
    (out,) = call(
        final_kernel,
        "vvvvvv",
        (inverse, far, *back),
        [((rhs, leaves * size), F32)],
        [pltpu.VMEM(panels.shape, F32), dma((4,))],
        out_space=hbm,
    )
    return out


def solution(mesh):
    return jax.shard_map(
        local,
        mesh=mesh,
        in_specs=(
            P("vec", "leaf"),
            P("leaf", None, "vec", None),
            P("leaf", None),
            P("leaf", None),
            P("leaf", None, None),
            P("leaf", None, None, None),
            P("leaf", None),
            P(),
            P(),
            P(),
        ),
        out_specs=P("vec", "leaf"),
        check_vma=False,
    )
```
